128 devices in a mesh: slab: 4 (over y), tile: 32 (over z, x, core).
Axes of the slice: x: 4, y: 4, z: 4, core: 2. Of those that a mesh axis runs over, the one named last changes fastest.
Arguments:
- coarse: bfloat16 [1048576, 256], P(('slab', 'tile')), may hold values from -6 to 6
- counts: int32 [128], P(('slab', 'tile')), may hold values from 1 to 1024, 65536 in all
- subdivided: int32 [128, 1024], P(('slab', 'tile')), may hold values from 0 to 8191, as said below
- requested: int32 [128, 128, 8], P(('slab', 'tile')), may hold values from -1 to 511, as said below
- neighbours: int32 [26, 65536], P(None, ('slab', 'tile')), may hold values from 0 to 1536
- up_weight: bfloat16 [256, 1024], replicated, may hold values from -0.375 to 0.375
- first_conv: bfloat16 [3456, 128], replicated, may hold values from -0.109375 to 0.109375
- second_conv: bfloat16 [3456, 128], replicated, may hold values from -0.109375 to 0.109375
- occupancy_weight: bfloat16 [128], replicated, may hold values from -0.5 to 0.5
Outputs:
- features: bfloat16 [65536, 1024], P(('slab', 'tile'))
- occupancy: float32 [8, 65536], P(None, ('slab', 'tile'))
The draws below stay inside these ranges and needn't reach their ends.
Inputs may be any that keep to these rules, and one draw needn't show every extreme that they name: The counts sum to 65536. `subdivided`: row h holds distinct cells of home device h; only its first counts[h] entries are read. requested[d, p, :] holds distinct slots of device p, then -1 for unused entries; every device reads 8 blocks from some other device; requested[d, d, :] is all -1.
All inputs are finite; a program needn't handle non-finite values.
Results may differ from the reference program's by a relative error of at most 0.0054.
Values may be sent and summed in bfloat16 or wider, within the bound.
No kernel may reach another device: no remote copies, remote signals or barrier semaphores. Data moves between devices by JAX's collectives and lax.ppermute only.
A program may use at most 128 MiB of HBM per device.

```python
import math
import jax
import jax.numpy as jnp
import numpy as np
from jax import lax

C = 256
CH = 128
CELLS_DEV = 8192
BLK_DEV = 512
REMOTE_DEV = 1024
CELLS = 1048576
BLOCKS = 65536
MAXSUB = 1024
NCAP = 8
DEVICES = 128


def draw_subdivided(key, part):
    home_keys = jax.random.split(key, DEVICES)

    def one_home(home_key):
        return jax.random.permutation(home_key, CELLS_DEV)[:MAXSUB].astype(jnp.int32)
    return jax.vmap(one_home)(home_keys)


def draw_requested(key, part):
    key_count, key_full, key_slots = jax.random.split(jax.random.fold_in(key, 7), 3)
    least = max(1, NCAP - NCAP // 4)
    drawn_counts = jax.random.randint(key_count, (DEVICES, DEVICES), least, NCAP + 1)
    lifted = jax.random.randint(key_full, (DEVICES,), 1, DEVICES)
    askers = jnp.arange(DEVICES, dtype=jnp.int32)
    full_peer = (askers + lifted) % DEVICES
    drawn_counts = jnp.where(askers[None, :] == full_peer[:, None], NCAP, drawn_counts)
    drawn_counts = jnp.where(askers[:, None] == askers[None, :], 0, drawn_counts)
    slot_keys = jax.random.split(key_slots, DEVICES * DEVICES)

    def one_pair(pair_key):
        return jax.random.permutation(pair_key, BLK_DEV)[:NCAP].astype(jnp.int32)
    slots = jax.vmap(one_pair)(slot_keys).reshape(DEVICES, DEVICES, NCAP)
    position = jnp.arange(NCAP, dtype=jnp.int32)
    return jnp.where(position[None, None, :] < drawn_counts[:, :, None], slots, -1).astype(jnp.int32)


def place_ends(entries, stream_key, smallest, largest):
    index_at = [jax.random.randint(jax.random.fold_in(stream_key, axis), (), 0, length) for axis, length in enumerate(entries.shape)]
    main_axis = entries.shape.index(max(entries.shape))
    next_to = index_at[:main_axis] + [(index_at[main_axis] + 1) % entries.shape[main_axis]] + index_at[main_axis + 1:]
    return entries.at[tuple(index_at)].set(smallest).at[tuple(next_to)].set(largest)


def block_levels(key, extent, cuts, smallest, largest):
    gain, own = 1.0, jax.random.fold_in(key, 6)
    for dim, parts in cuts:
        steps = jnp.exp(jax.random.uniform(jax.random.fold_in(own, dim), (parts,), jnp.float32, smallest / len(cuts), largest / len(cuts)))
        gain = gain * jnp.repeat(steps, extent[dim] // parts).reshape([-1 if axis == dim else 1 for axis in range(len(extent))])
    return gain


def split_up(count, total, most, slope):
    portions = [(1 << 20) // math.isqrt(standing ** slope) + 1 for standing in range(2, count + 1)]
    surplus, given = total - most - (count - 1), [1] * (count - 1)
    while surplus > 0:
        candidates = [i for i in range(count - 1) if given[i] < most]
        mass, budget = sum([portions[i] for i in candidates]), surplus
        for i in candidates:
            more = min(most - given[i], max(1, budget * portions[i] // mass), surplus)
            given[i] = given[i] + more
            surplus = surplus - more
    return np.array([most] + given)


def uneven(own_key, number_of, total, limit, lean):
    if number_of == 2:
        one = jax.random.randint(own_key, (), max(1, total - limit), min(limit, total - 1) + 1)
        return jnp.stack([one, total - one])
    tallies = jnp.asarray(split_up(number_of, total, limit, lean), jnp.int32)
    couples = (number_of - 1) // 2
    donor, sink = tallies[1:1 + 2 * couples:2], tallies[2:2 + 2 * couples:2]
    room = jnp.minimum(donor - 1, limit - sink)
    shifted = jax.random.randint(jax.random.fold_in(own_key, 1), (couples,), 0, 1 << 20) % (room + 1)
    tallies = tallies.at[1:1 + 2 * couples:2].set(donor - shifted).at[2:2 + 2 * couples:2].set(sink + shifted)
    return tallies[jax.random.permutation(jax.random.fold_in(own_key, 2), number_of)]


def bell_draw(key, extent, width, most, cuts=(), kind=jnp.bfloat16):
    loudness = block_levels(key, extent, cuts, -0.22, 0.18) if cuts else 1.0
    entries = jax.random.normal(key, extent, jnp.float32) * width * loudness
    return jnp.minimum(jnp.maximum(entries, -most), most).astype(kind)


def setup_inputs(seed: int = 0) -> dict:
    key_of = jax.random.split(jax.random.key(seed), 10)
    return {
        "coarse": bell_draw(key_of[0], (CELLS, C), 1.0, 6.0, ((0, 128),)),
        "counts": uneven(key_of[1], DEVICES, BLOCKS, MAXSUB, 2).astype(jnp.int32),
        "subdivided": draw_subdivided(jax.random.fold_in(key_of[9], 71), 0),
        "requested": draw_requested(jax.random.fold_in(key_of[9], 71), 0),
        "neighbours": place_ends(jax.random.randint(key_of[4], (26, BLOCKS), 0, BLK_DEV + REMOTE_DEV + 1), jax.random.fold_in(key_of[4], 1), 0, BLK_DEV + REMOTE_DEV).astype(jnp.int32),
        "up_weight": bell_draw(key_of[5], (C, 8 * CH), C ** -0.5, 0.375),
        "first_conv": bell_draw(key_of[6], (27 * CH, CH), (27 * CH) ** -0.5, 0.109375),
        "second_conv": bell_draw(key_of[7], (27 * CH, CH), (27 * CH) ** -0.5, 0.109375),
        "occupancy_weight": bell_draw(key_of[8], (CH,), CH ** -0.5, 0.5),
    }


def patch_tables():
    tap_list = []
    child_list = []
    for near_x in range(4):
        for near_y in range(4):
            for near_z in range(4):
                axis_parts = [((corner - 1) // 2, (corner - 1) % 2) for corner in (near_x, near_y, near_z)]
                tap_list.append((axis_parts[0][0] + 1) * 9 + (axis_parts[1][0] + 1) * 3 + axis_parts[2][0] + 1)
                child_list.append(axis_parts[0][1] * 4 + axis_parts[1][1] * 2 + axis_parts[2][1])
    return np.array(tap_list, np.int32), np.array(child_list, np.int32)


def spread_patch(patch_rows):
    pieces = []
    for start_x in range(3):
        for start_y in range(3):
            for start_z in range(3):
                pieces.append(patch_rows[:, start_x:start_x + 2, start_y:start_y + 2, start_z:start_z + 2, :])
    stacked = jnp.concatenate(pieces, axis=-1)
    return stacked.reshape(-1, 27 * patch_rows.shape[-1])


def convolve(source_table, rows_all, weight, group_size):
    channels = weight.shape[1]
    flat_table = source_table.reshape(-1, channels)
    tap_table, child_table = patch_tables()
    batches = rows_all.shape[0] // group_size

    def one_group(group_rows):
        flat_index = group_rows[:, tap_table] * 8 + child_table[None, :]
        patch_rows = flat_table[flat_index].reshape(group_size, 4, 4, 4, channels)
        result = jnp.dot(spread_patch(patch_rows), weight, preferred_element_type=jnp.float32)
        return result.reshape(group_size, 8 * channels)

    outputs = lax.map(one_group, rows_all.reshape(batches, group_size, 27))
    return outputs.reshape(-1, 8 * channels)


def reference(coarse, counts, subdivided, requested, neighbours, up_weight, first_conv, second_conv, occupancy_weight):
    storage = jnp.arange(BLOCKS, dtype=jnp.int32)
    owner_index = storage // BLK_DEV
    block_slot = storage % BLK_DEV
    upper_end = jnp.cumsum(counts, dtype=jnp.int32)
    lower_end = upper_end - counts
    block_rank = block_slot * DEVICES + owner_index
    home_index = jnp.sum((upper_end[None, :] <= block_rank[:, None]).astype(jnp.int32), axis=1, dtype=jnp.int32)
    cell_index = subdivided[home_index, block_rank - lower_end[home_index]]
    parent = coarse[home_index * CELLS_DEV + cell_index]
    children = jax.nn.silu(jnp.dot(parent, up_weight, preferred_element_type=jnp.float32)).astype(jnp.bfloat16)

    local_hit = neighbours < BLK_DEV
    remote = neighbours - BLK_DEV
    remote_hit = (remote >= 0) & (remote < DEVICES * NCAP)
    safe_remote = jnp.clip(remote, 0, DEVICES * NCAP - 1)
    peer_index = safe_remote // NCAP
    flat_need = requested.reshape(DEVICES, DEVICES * NCAP)
    slot_there = flat_need[owner_index[None, :], safe_remote]
    remote_ids = jnp.where(slot_there >= 0, peer_index * BLK_DEV + slot_there, BLOCKS)
    global_ids = jnp.where(local_hit, owner_index[None, :] * BLK_DEV + neighbours, jnp.where(remote_hit, remote_ids, BLOCKS))
    global_ids = global_ids.astype(jnp.int32)
    rows_all = jnp.concatenate([global_ids.T[:, :13], storage[:, None], global_ids.T[:, 13:]], axis=1)

    def with_absent(source_table):
        return jnp.concatenate([source_table, jnp.zeros((1, source_table.shape[1]), source_table.dtype)], axis=0)

    hidden = jax.nn.silu(convolve(with_absent(children), rows_all, first_conv, BLK_DEV)).astype(jnp.bfloat16)
    summed = children.astype(jnp.float32) + convolve(with_absent(hidden), rows_all, second_conv, BLK_DEV)
    features = summed.astype(jnp.bfloat16)
    occupancy = jnp.einsum("bac,c->ab", features.reshape(BLOCKS, 8, CH), occupancy_weight, preferred_element_type=jnp.float32)
    return features, occupancy
```

```python
import functools

import jax
import jax.numpy as jnp
import numpy as np
from jax import lax
from jax.experimental import pallas as pl
from jax.experimental.pallas import tpu as pltpu
from jax.sharding import PartitionSpec as P

AXES = ("slab", "tile")
F32 = jnp.float32
BF16 = jnp.bfloat16
VMEM_LIMIT = 58 * 2**20
VM = pl.BlockSpec(memory_space=pltpu.VMEM)
SM = pl.BlockSpec(memory_space=pltpu.SMEM)
UNROLL = 64


def axis_children(offset):
    if offset == -1:
        return ([1], [0])
    if offset == 1:
        return ([0], [1])
    return ([0, 1], [0, 1])


def neighbour_plan():
    plans = []
    for near in np.ndindex(3, 3, 3):
        near = [v - 1 for v in near]
        parts = [axis_children(v) for v in near]
        sources = [(a, b, c) for a in parts[0][0] for b in parts[1][0] for c in parts[2][0]]
        targets = [(a, b, c) for a in parts[0][1] for b in parts[1][1] for c in parts[2][1]]
        taps = []
        for s in sources:
            row = []
            for t in targets:
                o = [2 * near[i] + s[i] - t[i] for i in range(3)]
                row.append(9 * (o[0] + 1) + 3 * (o[1] + 1) + o[2] + 1)
            taps.append(row)
        code = lambda v: 4 * v[0] + 2 * v[1] + v[2]
        plans.append(([code(s) for s in sources], [code(t) for t in targets], taps))
    return plans


PLANS = neighbour_plan()


def tap_block(w_ref, tap):
    return w_ref[tap * 128 : (tap + 1) * 128, :]


def tap_matrix(w_ref, taps):
    return jnp.concatenate(
        [jnp.concatenate([tap_block(w_ref, t) for t in row], axis=1) for row in taps], axis=0
    )


def dot(a, b):
    return jnp.dot(a, b, preferred_element_type=F32)


def convolve(idx_ref, own_ref, w_ref, table, picked, total):
    blocks = own_ref.shape[0]
    sources, targets, taps = PLANS[13]
    for pair in range(4):
        cols = tap_matrix(w_ref, [row[2 * pair : 2 * pair + 2] for row in taps])
        part = dot(own_ref[...], cols)
        total[2 * pair] = part[:, :128]
        total[2 * pair + 1] = part[:, 128:]
    for t in range(26):
        sources, targets, taps = PLANS[t if t < 13 else t + 1]

        def some_rows(i, carry, t=t):
            base = t * blocks + i * UNROLL
            at = pl.multiple_of(i * (UNROLL * 8), UNROLL * 8)
            rows = [
                table[pl.ds(pl.multiple_of(idx_ref[base + u], 8), 8), :] for u in range(UNROLL)
            ]
            for u in range(UNROLL):
                picked[pl.ds(at + u * 8, 8), :] = rows[u]
            return carry

        lax.fori_loop(0, blocks // UNROLL, some_rows, 0)
        left = jnp.concatenate(
            [picked[pl.ds(s, blocks, stride=8), :].astype(BF16) for s in sources], axis=1
        )
        step = min(2, len(targets))
        for j in range(0, len(targets), step):
            part = dot(left, tap_matrix(w_ref, [row[j : j + step] for row in taps]))
            for k in range(step):
                total[targets[j + k]] += part[:, k * 128 : (k + 1) * 128]


def silu(x):
    return x * jax.nn.sigmoid(x)


def roll_kernel(me_ref, got_ref, home_ref, out_ref):
    devices = got_ref.shape[0]
    me = me_ref[0]
    ids = lax.broadcasted_iota(jnp.int32, (devices, 1), 0)
    lower = jnp.sum(jnp.where(ids < me, got_ref[:, 8:9], 0))
    shift = lax.rem(lower, devices)

    def one(d, carry):
        src = lax.rem(d - shift + devices, devices)
        out_ref[d] = home_ref[src]
        return carry

    lax.fori_loop(0, devices, one, 0, unroll=8)


def select_rows(got_ref, source, scratch, out_ref):
    devices = got_ref.shape[0]
    blocks, width = source.shape
    lanes = lax.broadcasted_iota(jnp.int32, (devices, blocks), 1)
    for k in range(8):
        pick = (got_ref[:, k : k + 1] == lanes).astype(BF16)
        part = dot(pick, source)
        for c in range(width // 128):
            scratch[c, pl.ds(k, devices, stride=8), :] = part[:, c * 128 : (c + 1) * 128]
    for c in range(width // 128):
        out_ref[:, :, c * 128 : (c + 1) * 128] = (
            scratch[c].astype(BF16).reshape(devices, 8, 128)
        )


def parent_kernel(me_ref, got_ref, arrived_ref, parent_ref, send_ref, scratch):
    devices = got_ref.shape[0]
    blocks = parent_ref.shape[0]
    me = me_ref[0]
    cols = devices * 8
    home = lax.broadcasted_iota(jnp.int32, (devices, cols), 1) // 8
    row = lax.broadcasted_iota(jnp.int32, (devices, cols), 0)
    counts = got_ref[:, 8:9]
    lower = jnp.sum(jnp.where(row < home, counts, 0), axis=0, keepdims=True)
    upper = jnp.sum(jnp.where(row <= home, counts, 0), axis=0, keepdims=True)
    within = lax.broadcasted_iota(jnp.int32, (1, cols), 1) % 8
    slot = (lower - me + devices - 1) // devices + within
    slot = jnp.where(slot * devices + me < upper, slot, -1)
    pick = (lax.broadcasted_iota(jnp.int32, (blocks, cols), 0) == slot).astype(BF16)
    parent = dot(pick, arrived_ref[...]).astype(BF16)
    parent_ref[...] = parent
    select_rows(got_ref, parent, scratch, send_ref)


def first_kernel(
    idx_ref, got_ref, parent_ref, far_ref, up_ref, w_ref,
    child_ref, hidden_ref, send_ref, table, picked, total, scratch,
):
    blocks = parent_ref.shape[0]
    rows = 128

    def lift(parents, base):
        made = silu(dot(parents, up_ref[...])).astype(BF16)
        for q in range(8):
            table[pl.ds(base * 8 + q, rows, stride=8), :] = (
                made[:, q * 128 : (q + 1) * 128].astype(F32)
            )
        return made

    def own_rows(i, carry):
        at = pl.ds(pl.multiple_of(i * rows, rows), rows)
        child_ref[at, :] = lift(parent_ref[at, :], pl.multiple_of(i * rows, rows))
        return carry

    def far_rows(i, carry):
        at = pl.ds(pl.multiple_of(i * rows, rows), rows)
        lift(far_ref[at, :], pl.multiple_of(blocks + i * rows, rows))
        return carry

    lax.fori_loop(0, blocks // rows, own_rows, 0)
    lax.fori_loop(0, far_ref.shape[0] // rows, far_rows, 0)
    last = (blocks + far_ref.shape[0]) * 8
    table[last : last + 8, :] = jnp.zeros((8, 128), F32)
    convolve(idx_ref, child_ref, w_ref, table, picked, total)
    for q in range(8):
        hidden_ref[:, q * 128 : (q + 1) * 128] = silu(total[q]).astype(BF16)
    select_rows(got_ref, hidden_ref[...], scratch, send_ref)


def second_kernel(
    idx_ref, child_ref, hidden_ref, far_ref, w_ref, occ_ref,
    feature_ref, occupancy_ref, table, picked, total,
):
    blocks = hidden_ref.shape[0]
    rows = 128

    def fill(ref, base):
        def some(i, carry):
            at = pl.ds(pl.multiple_of(i * rows, rows), rows)
            to = pl.multiple_of((base + i * rows) * 8, rows * 8)
            for q in range(8):
                table[pl.ds(to + q, rows, stride=8), :] = (
                    ref[at, q * 128 : (q + 1) * 128].astype(F32)
                )
            return carry

        lax.fori_loop(0, ref.shape[0] // rows, some, 0)

    fill(hidden_ref, 0)
    far = far_ref.shape[0]
    fill(far_ref, blocks)
    last = (blocks + far) * 8
    table[last : last + 8, :] = jnp.zeros((8, 128), F32)
    convolve(idx_ref, hidden_ref, w_ref, table, picked, total)
    for q in range(8):
        at = slice(q * 128, (q + 1) * 128)
        feature_ref[:, at] = (child_ref[:, at].astype(F32) + total[q]).astype(BF16)
    lane = lax.broadcasted_iota(jnp.int32, (8, 1024), 1) // 128
    row = lax.broadcasted_iota(jnp.int32, (8, 1024), 0)
    head = jnp.where(lane == row, jnp.concatenate([occ_ref[...].astype(F32)] * 8, axis=1), 0.0)
    occupancy_ref[...] = lax.dot_general(
        head.astype(BF16), feature_ref[...], (((1,), (1,)), ((), ())), preferred_element_type=F32
    )


def shape(*dims, dtype=BF16):
    return jax.ShapeDtypeStruct(dims, dtype)


def call(kernel, out_shape, in_specs, scratch=()):
    return pl.pallas_call(
        kernel,
        out_shape=out_shape,
        in_specs=in_specs,
        out_specs=jax.tree.map(lambda _: VM, out_shape),
        scratch_shapes=list(scratch),
        compiler_params=pltpu.CompilerParams(vmem_limit_bytes=VMEM_LIMIT),
    )


def exchange(x):
    return lax.all_to_all(x, AXES, split_axis=0, concat_axis=0, tiled=True)


def body(
    coarse, counts, subdivided, requested, neighbours,
    up_weight, first_conv, second_conv, occupancy_weight,
):
    devices = lax.axis_size(AXES)
    me = lax.axis_index(AXES).astype(jnp.int32).reshape(1)
    blocks = neighbours.shape[1]
    far = devices * 8
    table_rows = (blocks + far + 8) * 8

    note = jnp.concatenate(
        [requested[0], jnp.broadcast_to(counts[:, None], (devices, 8))], axis=1
    )
    got = exchange(note.reshape(devices, 1, 16)).reshape(devices, 16)
    order = subdivided[0].reshape(8, devices).T.reshape(-1)
    home = coarse[order].reshape(devices, 8, -1)
    idx = (neighbours * 8).reshape(-1)

    leaving = call(roll_kernel, shape(devices, 8, 256), [SM, VM, VM])(me, got, home)
    arrived = exchange(leaving)
    parent, send = call(
        parent_kernel,
        (shape(blocks, 256), shape(devices, 8, 256)),
        [SM, VM, VM],
        [pltpu.VMEM((2, far, 128), F32)],
    )(me, got, arrived.reshape(far, 256))
    far_parent = exchange(send).reshape(far, 256)

    work = [
        pltpu.VMEM((table_rows, 128), F32),
        pltpu.VMEM((blocks * 8, 128), F32),
        pltpu.VMEM((8, blocks, 128), F32),
    ]
    child, hidden, send = call(
        first_kernel,
        (shape(blocks, 1024), shape(blocks, 1024), shape(devices, 8, 1024)),
        [SM] + [VM] * 5,
        work + [pltpu.VMEM((8, far, 128), F32)],
    )(idx, got, parent, far_parent, up_weight, first_conv)
    far_hidden = exchange(send).reshape(far, 1024)
    return tuple(
        call(
            second_kernel,
            (shape(blocks, 1024), shape(8, blocks, dtype=F32)),
            [SM] + [VM] * 5,
            work,
        )(idx, child, hidden, far_hidden, second_conv, occupancy_weight.reshape(1, 128))
    )


def solution(mesh):
    rows = P(AXES, None)
    in_specs = (rows, P(AXES), rows, P(AXES, None, None), P(None, AXES), P(), P(), P(), P())
    out_specs = (rows, P(None, AXES))
    return jax.shard_map(body, mesh=mesh, in_specs=in_specs, out_specs=out_specs, check_vma=False)
```

```python
import functools

import jax
import jax.numpy as jnp
import numpy as np
from jax import lax
from jax.experimental import pallas as pl
from jax.experimental.pallas import tpu as pltpu
from jax.sharding import PartitionSpec as P

AXES = ("slab", "tile")
F32 = jnp.float32
BF16 = jnp.bfloat16
VMEM_LIMIT = 58 * 2**20
VM = pl.BlockSpec(memory_space=pltpu.VMEM)
SM = pl.BlockSpec(memory_space=pltpu.SMEM)
GROUP = 32


def axis_children(offset):
    if offset == -1:
        return ([1], [0])
    if offset == 1:
        return ([0], [1])
    return ([0, 1], [0, 1])


def neighbour_plan():
    plans = []
    for near in np.ndindex(3, 3, 3):
        near = [v - 1 for v in near]
        parts = [axis_children(v) for v in near]
        sources = [(a, b, c) for a in parts[0][0] for b in parts[1][0] for c in parts[2][0]]
        targets = [(a, b, c) for a in parts[0][1] for b in parts[1][1] for c in parts[2][1]]
        taps = []
        for s in sources:
            row = []
            for t in targets:
                o = [2 * near[i] + s[i] - t[i] for i in range(3)]
                row.append(9 * (o[0] + 1) + 3 * (o[1] + 1) + o[2] + 1)
            taps.append(row)
        code = lambda v: 4 * v[0] + 2 * v[1] + v[2]
        plans.append(([code(s) for s in sources], [code(t) for t in targets], taps))
    return plans


PLANS = neighbour_plan()


def tap_block(w_ref, tap):
    return w_ref[tap * 128 : (tap + 1) * 128, :]


def tap_matrix(w_ref, taps):
    return jnp.concatenate(
        [jnp.concatenate([tap_block(w_ref, t) for t in row], axis=1) for row in taps], axis=0
    )


def dot(a, b):
    return jnp.dot(a, b, preferred_element_type=F32)


def convolve(idx_ref, own_ref, w_ref, table, picked, total):
    blocks = own_ref.shape[0]

    def pick(t):
        into = picked[t % 2]
        for first in range(t * blocks, (t + 1) * blocks, GROUP):
            rows = [
                table[pl.ds(pl.multiple_of(idx_ref[first + u], 8), 8), :] for u in range(GROUP)
            ]
            at = (first - t * blocks) * 8
            for u in range(GROUP):
                into[at + u * 8 : at + u * 8 + 8, :] = rows[u]

    def add(left, plan, fresh):
        sources, targets, taps = plan
        step = min(2, len(targets))
        for j in range(0, len(targets), step):
            part = dot(left, tap_matrix(w_ref, [row[j : j + step] for row in taps]))
            for k in range(step):
                piece = part[:, k * 128 : (k + 1) * 128]
                if fresh:
                    total[targets[j + k]] = piece
                else:
                    total[targets[j + k]] += piece

    for t in range(-1, 26):

        def step(i, carry, t=t):
            if t + 1 < 26:
                pick(t + 1)
            if t < 0:
                add(own_ref[...], PLANS[13], True)
            else:
                plan = PLANS[t if t < 13 else t + 1]
                near = picked[t % 2]
                left = [near[pl.ds(s, blocks, stride=8), :].astype(BF16) for s in plan[0]]
                add(jnp.concatenate(left, axis=1), plan, False)
            return carry

        lax.fori_loop(0, 1, step, 0)


def silu(x):
    return x * jax.nn.sigmoid(x)


def roll_kernel(me_ref, got_ref, home_ref, out_ref):
    devices = got_ref.shape[0]
    me = me_ref[0]
    ids = lax.broadcasted_iota(jnp.int32, (devices, 1), 0)
    lower = jnp.sum(jnp.where(ids < me, got_ref[:, 8:9], 0))
    shift = lax.rem(lower, devices)

    def one(d, carry):
        src = lax.rem(d - shift + devices, devices)
        out_ref[d] = home_ref[src]
        return carry

    lax.fori_loop(0, devices, one, 0, unroll=8)


def select_rows(got_ref, source, scratch, out_ref):
    devices = got_ref.shape[0]
    blocks, width = source.shape
    lanes = lax.broadcasted_iota(jnp.int32, (devices, blocks), 1)
    for k in range(8):
        pick = (got_ref[:, k : k + 1] == lanes).astype(BF16)
        part = dot(pick, source)
        for c in range(width // 128):
            scratch[c, pl.ds(k, devices, stride=8), :] = part[:, c * 128 : (c + 1) * 128]
    for c in range(width // 128):
        out_ref[:, :, c * 128 : (c + 1) * 128] = (
            scratch[c].astype(BF16).reshape(devices, 8, 128)
        )


def parent_kernel(me_ref, got_ref, arrived_ref, parent_ref, send_ref, scratch):
    devices = got_ref.shape[0]
    blocks = parent_ref.shape[0]
    me = me_ref[0]
    cols = devices * 8
    home = lax.broadcasted_iota(jnp.int32, (devices, cols), 1) // 8
    row = lax.broadcasted_iota(jnp.int32, (devices, cols), 0)
    counts = got_ref[:, 8:9]
    lower = jnp.sum(jnp.where(row < home, counts, 0), axis=0, keepdims=True)
    upper = jnp.sum(jnp.where(row <= home, counts, 0), axis=0, keepdims=True)
    within = lax.broadcasted_iota(jnp.int32, (1, cols), 1) % 8
    slot = (lower - me + devices - 1) // devices + within
    slot = jnp.where(slot * devices + me < upper, slot, -1)
    pick = (lax.broadcasted_iota(jnp.int32, (blocks, cols), 0) == slot).astype(BF16)
    parent = dot(pick, arrived_ref[...]).astype(BF16)
    parent_ref[...] = parent
    select_rows(got_ref, parent, scratch, send_ref)


def first_kernel(
    idx_ref, got_ref, parent_ref, far_ref, up_ref, w_ref,
    child_ref, hidden_ref, send_ref, table, picked, total, scratch,
):
    blocks = parent_ref.shape[0]
    rows = 128

    def lift(parents, base):
        made = silu(dot(parents, up_ref[...])).astype(BF16)
        for q in range(8):
            table[pl.ds(base * 8 + q, rows, stride=8), :] = (
                made[:, q * 128 : (q + 1) * 128].astype(F32)
            )
        return made

    def own_rows(i, carry):
        at = pl.ds(pl.multiple_of(i * rows, rows), rows)
        child_ref[at, :] = lift(parent_ref[at, :], pl.multiple_of(i * rows, rows))
        return carry

    def far_rows(i, carry):
        at = pl.ds(pl.multiple_of(i * rows, rows), rows)
        lift(far_ref[at, :], pl.multiple_of(blocks + i * rows, rows))
        return carry

    lax.fori_loop(0, blocks // rows, own_rows, 0)
    lax.fori_loop(0, far_ref.shape[0] // rows, far_rows, 0)
    last = (blocks + far_ref.shape[0]) * 8
    table[last : last + 8, :] = jnp.zeros((8, 128), F32)
    convolve(idx_ref, child_ref, w_ref, table, picked, total)
    for q in range(8):
        hidden_ref[:, q * 128 : (q + 1) * 128] = silu(total[q]).astype(BF16)
    select_rows(got_ref, hidden_ref[...], scratch, send_ref)


def second_kernel(
    idx_ref, child_ref, hidden_ref, far_ref, w_ref, occ_ref,
    feature_ref, occupancy_ref, table, picked, total,
):
    blocks = hidden_ref.shape[0]
    rows = 128

    def fill(ref, base):
        def some(i, carry):
            at = pl.ds(pl.multiple_of(i * rows, rows), rows)
            to = pl.multiple_of((base + i * rows) * 8, rows * 8)
            for q in range(8):
                table[pl.ds(to + q, rows, stride=8), :] = (
                    ref[at, q * 128 : (q + 1) * 128].astype(F32)
                )
            return carry

        lax.fori_loop(0, ref.shape[0] // rows, some, 0)

    fill(hidden_ref, 0)
    far = far_ref.shape[0]
    fill(far_ref, blocks)
    last = (blocks + far) * 8
    table[last : last + 8, :] = jnp.zeros((8, 128), F32)
    convolve(idx_ref, hidden_ref, w_ref, table, picked, total)
    for q in range(8):
        at = slice(q * 128, (q + 1) * 128)
        feature_ref[:, at] = (child_ref[:, at].astype(F32) + total[q]).astype(BF16)
    lane = lax.broadcasted_iota(jnp.int32, (8, 1024), 1) // 128
    row = lax.broadcasted_iota(jnp.int32, (8, 1024), 0)
    head = jnp.where(lane == row, jnp.concatenate([occ_ref[...].astype(F32)] * 8, axis=1), 0.0)
    occupancy_ref[...] = lax.dot_general(
        head.astype(BF16), feature_ref[...], (((1,), (1,)), ((), ())), preferred_element_type=F32
    )


def shape(*dims, dtype=BF16):
    return jax.ShapeDtypeStruct(dims, dtype)


def call(kernel, out_shape, in_specs, scratch=()):
    return pl.pallas_call(
        kernel,
        out_shape=out_shape,
        in_specs=in_specs,
        out_specs=jax.tree.map(lambda _: VM, out_shape),
        scratch_shapes=list(scratch),
        compiler_params=pltpu.CompilerParams(vmem_limit_bytes=VMEM_LIMIT),
    )


def exchange(x):
    return lax.all_to_all(x, AXES, split_axis=0, concat_axis=0, tiled=True)


def body(
    coarse, counts, subdivided, requested, neighbours,
    up_weight, first_conv, second_conv, occupancy_weight,
):
    devices = lax.axis_size(AXES)
    me = lax.axis_index(AXES).astype(jnp.int32).reshape(1)
    blocks = neighbours.shape[1]
    far = devices * 8
    table_rows = (blocks + far + 8) * 8

    note = jnp.concatenate(
        [requested[0], jnp.broadcast_to(counts[:, None], (devices, 8))], axis=1
    )
    got = exchange(note.reshape(devices, 1, 16)).reshape(devices, 16)
    order = subdivided[0].reshape(8, devices).T.reshape(-1)
    home = coarse[order].reshape(devices, 8, -1)
    idx = (neighbours * 8).reshape(-1)

    leaving = call(roll_kernel, shape(devices, 8, 256), [SM, VM, VM])(me, got, home)
    arrived = exchange(leaving)
    parent, send = call(
        parent_kernel,
        (shape(blocks, 256), shape(devices, 8, 256)),
        [SM, VM, VM],
        [pltpu.VMEM((2, far, 128), F32)],
    )(me, got, arrived.reshape(far, 256))
    far_parent = exchange(send).reshape(far, 256)

    work = [
        pltpu.VMEM((table_rows, 128), F32),
        (pltpu.VMEM((blocks * 8, 128), F32),) * 2,
        pltpu.VMEM((8, blocks, 128), F32),
    ]
    child, hidden, send = call(
        first_kernel,
        (shape(blocks, 1024), shape(blocks, 1024), shape(devices, 8, 1024)),
        [SM] + [VM] * 5,
        work + [pltpu.VMEM((8, far, 128), F32)],
    )(idx, got, parent, far_parent, up_weight, first_conv)
    far_hidden = exchange(send).reshape(far, 1024)
    return tuple(
        call(
            second_kernel,
            (shape(blocks, 1024), shape(8, blocks, dtype=F32)),
            [SM] + [VM] * 5,
            work,
        )(idx, child, hidden, far_hidden, second_conv, occupancy_weight.reshape(1, 128))
    )


def solution(mesh):
    rows = P(AXES, None)
    in_specs = (rows, P(AXES), rows, P(AXES, None, None), P(None, AXES), P(), P(), P(), P())
    out_specs = (rows, P(None, AXES))
    return jax.shard_map(body, mesh=mesh, in_specs=in_specs, out_specs=out_specs, check_vma=False)
```

```python
import functools

import jax
import jax.numpy as jnp
import numpy as np
from jax import lax
from jax.experimental import pallas as pl
from jax.experimental.pallas import tpu as pltpu
from jax.sharding import PartitionSpec as P

AXES = ("slab", "tile")
F32 = jnp.float32
BF16 = jnp.bfloat16
VMEM_LIMIT = 58 * 2**20
SMALL = 16 * 2**20
VM = pl.BlockSpec(memory_space=pltpu.VMEM)
ANY = pl.BlockSpec(memory_space=pl.ANY)
GROUP = 32


def axis_children(offset):
    if offset == -1:
        return ([1], [0])
    if offset == 1:
        return ([0], [1])
    return ([0, 1], [0, 1])


def neighbour_plan():
    plans = []
    for near in np.ndindex(3, 3, 3):
        near = [v - 1 for v in near]
        parts = [axis_children(v) for v in near]
        sources = [(a, b, c) for a in parts[0][0] for b in parts[1][0] for c in parts[2][0]]
        targets = [(a, b, c) for a in parts[0][1] for b in parts[1][1] for c in parts[2][1]]
        taps = []
        for s in sources:
            row = []
            for t in targets:
                o = [2 * near[i] + s[i] - t[i] for i in range(3)]
                row.append(9 * (o[0] + 1) + 3 * (o[1] + 1) + o[2] + 1)
            taps.append(row)
        code = lambda v: 4 * v[0] + 2 * v[1] + v[2]
        plans.append(([code(s) for s in sources], [code(t) for t in targets], taps))
    return plans


PLANS = neighbour_plan()


def tap_block(w_ref, tap):
    return w_ref[tap * 128 : (tap + 1) * 128, :]


def tap_matrix(w_ref, taps):
    return jnp.concatenate(
        [jnp.concatenate([tap_block(w_ref, t) for t in row], axis=1) for row in taps], axis=0
    )


def dot(a, b):
    return jnp.dot(a, b, preferred_element_type=F32)


def add_dots(left, plan, w_ref, total, fresh=False):
    sources, targets, taps = plan
    step = min(2, len(targets))
    for j in range(0, len(targets), step):
        part = dot(left, tap_matrix(w_ref, [row[j : j + step] for row in taps]))
        for k in range(step):
            piece = part[:, k * 128 : (k + 1) * 128]
            if fresh:
                total[targets[j + k]] = piece
            else:
                total[targets[j + k]] += piece


def add_neighbours(idx_ref, w_ref, table, picked, total):
    blocks = total.shape[1]

    def pick(t):
        into = picked[t % 2]
        for first in range(t * blocks, (t + 1) * blocks, GROUP):
            rows = [
                table[pl.ds(pl.multiple_of(idx_ref[first + u], 8), 8), :] for u in range(GROUP)
            ]
            at = (first - t * blocks) * 8
            for u in range(GROUP):
                into[at + u * 8 : at + u * 8 + 8, :] = rows[u]

    for t in range(-1, 26):

        def step(i, carry, t=t):
            if t + 1 < 26:
                pick(t + 1)
            if t >= 0:
                plan = PLANS[t if t < 13 else t + 1]
                near = picked[t % 2]
                left = [near[pl.ds(s, blocks, stride=8), :].astype(BF16) for s in plan[0]]
                add_dots(jnp.concatenate(left, axis=1), plan, w_ref, total)
            return carry

        lax.fori_loop(0, 1, step, 0)


def copies(pairs, sems):
    made = [pltpu.make_async_copy(a, b, sems.at[i]) for i, (a, b) in enumerate(pairs)]
    for copy in made:
        copy.start()
    return made


def fill_table(table, ref, base):
    rows = 128

    def some(i, carry):
        at = pl.ds(pl.multiple_of(i * rows, rows), rows)
        to = pl.multiple_of((base + i * rows) * 8, rows * 8)
        for q in range(8):
            table[pl.ds(to + q, rows, stride=8), :] = (
                ref[at, q * 128 : (q + 1) * 128].astype(F32)
            )
        return carry

    lax.fori_loop(0, ref.shape[0] // rows, some, 0)


def silu(x):
    return x * jax.nn.sigmoid(x)


def home_kernel(sub_ref, coarse_ref, out_ref, place, raw, wide, rows, sems):
    devices = out_ref.shape[0]
    cells = coarse_ref.shape[0]
    part = cells // 4
    spot = pltpu.make_async_copy(sub_ref, place, sems.at[4])
    spot.start()
    loads = copies(
        [(coarse_ref.at[pl.ds(i * part, part)], raw.at[pl.ds(i * part, part)]) for i in range(4)],
        sems,
    )
    for i in range(4):
        loads[i].wait()

        def widen(j, carry, i=i):
            at = pl.ds(pl.multiple_of(i * part + j * 128, 128), 128)
            for half in range(2):
                wide[half, at, :] = raw[at, half * 128 : (half + 1) * 128].astype(F32)
            return carry

        lax.fori_loop(0, part // 128, widen, 0, unroll=2)
    spot.wait()

    def some(i, carry):
        first = i * 32
        k = first // devices
        to = lax.rem(first, devices) * 8 + k
        cells_here = [place[0, first + u] for u in range(32)]
        for half in range(2):
            got = [wide[half, pl.ds(c, 1), :] for c in cells_here]
            for u in range(32):
                rows[half, pl.ds(to + u * 8, 1), :] = got[u]
        return carry

    lax.fori_loop(0, devices * 8 // 32, some, 0)
    for half in range(2):
        out_ref[:, :, half * 128 : (half + 1) * 128] = (
            rows[half].astype(BF16).reshape(devices, 8, 128)
        )


def own_index():
    return lax.axis_index(AXES[0]) * lax.axis_size(AXES[1]) + lax.axis_index(AXES[1])


def roll_kernel(got_ref, home_ref, out_ref):
    devices = got_ref.shape[0]
    me = own_index()
    ids = lax.broadcasted_iota(jnp.int32, (devices, 1), 0)
    lower = jnp.sum(jnp.where(ids < me, got_ref[:, 8:9], 0))
    shift = lax.rem(lower, devices)

    def one(d, carry):
        src = lax.rem(d - shift + devices, devices)
        out_ref[d] = home_ref[src]
        return carry

    lax.fori_loop(0, devices, one, 0, unroll=8)


def select_rows(got_ref, source, scratch, out_ref, done=None):
    devices = got_ref.shape[0]
    blocks, width = source.shape
    lanes = lax.broadcasted_iota(jnp.int32, (devices, blocks), 1)
    pick = jnp.concatenate(
        [(got_ref[:, k : k + 1] == lanes).astype(BF16) for k in range(8)], axis=0
    )
    for c in range(0, width, 256):
        part = dot(pick, source[:, c : c + 256])
        for half in range(2):
            to = scratch.at[half]
            for k in range(8):
                to[pl.ds(k, devices, stride=8), :] = (
                    part[k * devices : (k + 1) * devices, half * 128 : (half + 1) * 128]
                )
            at = c + half * 128
            out_ref[:, :, at : at + 128] = to[...].astype(BF16).reshape(devices, 8, 128)
        if done is not None:
            done(c // 256, pl.ds(c, 256))


def parent_kernel(got_ref, arrived_ref, parent_ref, send_ref, scratch):
    devices = got_ref.shape[0]
    blocks = parent_ref.shape[0]
    me = own_index()
    cols = devices * 8
    home = lax.broadcasted_iota(jnp.int32, (devices, cols), 1) // 8
    row = lax.broadcasted_iota(jnp.int32, (devices, cols), 0)
    counts = got_ref[:, 8:9]
    lower = jnp.sum(jnp.where(row < home, counts, 0), axis=0, keepdims=True)
    upper = jnp.sum(jnp.where(row <= home, counts, 0), axis=0, keepdims=True)
    within = lax.broadcasted_iota(jnp.int32, (1, cols), 1) % 8
    slot = (lower - me + devices - 1) // devices + within
    slot = jnp.where(slot * devices + me < upper, slot, -1)
    pick = (lax.broadcasted_iota(jnp.int32, (blocks, cols), 0) == slot).astype(BF16)
    parent = dot(pick, arrived_ref[...]).astype(BF16)
    parent_ref[...] = parent
    select_rows(got_ref, parent, scratch, send_ref)


def own_kernel(parent_ref, up_ref, w_ref, child_ref, total_ref):
    child_ref[...] = silu(dot(parent_ref[...], up_ref[...])).astype(BF16)
    add_dots(child_ref[...], PLANS[13], w_ref, total_ref, fresh=True)


def own_second_kernel(child_ref, hidden_ref, w_ref, total_ref):
    add_dots(hidden_ref[...], PLANS[13], w_ref, total_ref, fresh=True)
    for q in range(8):
        total_ref[q] += child_ref[:, q * 128 : (q + 1) * 128].astype(F32)


def first_kernel(
    idx_ref, got_ref, child_ref, far_ref, up_ref, w_ref, total_ref,
    hidden_ref, send_ref,
    table, picked, total, idx, w, child, scratch, hidden, send, sems,
):
    blocks = child_ref.shape[0]
    far = far_ref.shape[0]
    rows = 512
    loads = copies(
        [(child_ref, child), (idx_ref, idx), (w_ref, w), (total_ref, total)], sems
    )

    def far_rows(i, carry):
        at = pl.ds(pl.multiple_of(i * rows, rows), rows)
        to = pl.multiple_of((blocks + i * rows) * 8, 8)
        made = silu(dot(far_ref[at, :], up_ref[...])).astype(BF16)
        for q in range(8):
            table[pl.ds(to + q, rows, stride=8), :] = made[:, q * 128 : (q + 1) * 128].astype(F32)
        return carry

    lax.fori_loop(0, far // rows, far_rows, 0)
    last = (blocks + far) * 8
    table[last : last + 8, :] = jnp.zeros((8, 128), F32)
    loads[0].wait()
    fill_table(table, child, 0)
    for load in loads[1:]:
        load.wait()
    add_neighbours(idx, w, table, picked, total)
    for q in range(8):
        hidden[:, q * 128 : (q + 1) * 128] = silu(total[q]).astype(BF16)
    leaving = [pltpu.make_async_copy(hidden, hidden_ref, sems.at[4])]
    leaving[0].start()

    def send_columns(number, columns):
        copy = pltpu.make_async_copy(
            send.at[:, :, columns], send_ref.at[:, :, columns], sems.at[5 + number]
        )
        copy.start()
        leaving.append(copy)

    select_rows(got_ref, hidden, scratch, send, send_columns)
    for copy in leaving:
        copy.wait()


def second_kernel(
    idx_ref, hidden_ref, far_ref, w_ref, total_ref, occ_ref,
    feature_ref, occupancy_ref,
    table, picked, total, idx, w, hidden, far, sems,
):
    blocks = hidden_ref.shape[0]
    rows = far_ref.shape[0]
    half = rows // 2
    loads = copies(
        [
            (hidden_ref, hidden),
            (far_ref.at[pl.ds(0, half)], far.at[pl.ds(0, half)]),
            (far_ref.at[pl.ds(half, half)], far.at[pl.ds(half, half)]),
            (idx_ref, idx),
            (w_ref, w),
            (total_ref, total),
        ],
        sems,
    )
    last = (blocks + rows) * 8
    table[last : last + 8, :] = jnp.zeros((8, 128), F32)
    loads[0].wait()
    fill_table(table, hidden, 0)
    for part in range(2):
        loads[1 + part].wait()
        fill_table(table, far.at[pl.ds(part * half, half)], blocks + part * half)
    for load in loads[3:]:
        load.wait()
    add_neighbours(idx, w, table, picked, total)
    for q in range(8):
        feature_ref[:, q * 128 : (q + 1) * 128] = total[q].astype(BF16)
    lane = lax.broadcasted_iota(jnp.int32, (8, 1024), 1) // 128
    row = lax.broadcasted_iota(jnp.int32, (8, 1024), 0)
    head = jnp.where(lane == row, jnp.concatenate([occ_ref[...].astype(F32)] * 8, axis=1), 0.0)
    occupancy_ref[...] = lax.dot_general(
        head.astype(BF16), feature_ref[...], (((1,), (1,)), ((), ())), preferred_element_type=F32
    )


def shape(*dims, dtype=BF16):
    return jax.ShapeDtypeStruct(dims, dtype)


def call(kernel, out_shape, in_specs, scratch=(), out_specs=None, flops=0, limit=VMEM_LIMIT):
    return pl.pallas_call(
        kernel,
        out_shape=out_shape,
        in_specs=in_specs,
        out_specs=out_specs or jax.tree.map(lambda _: VM, out_shape),
        scratch_shapes=list(scratch),
        compiler_params=pltpu.CompilerParams(vmem_limit_bytes=limit),
        cost_estimate=pl.CostEstimate(flops=flops, bytes_accessed=4 * 2**20, transcendentals=0),
    )


def exchange(x):
    return lax.all_to_all(x, AXES, split_axis=0, concat_axis=0, tiled=True)


def body(
    coarse, counts, subdivided, requested, neighbours,
    up_weight, first_conv, second_conv, occupancy_weight,
):
    devices = lax.axis_size(AXES)
    blocks = neighbours.shape[1]
    far = devices * 8
    table_rows = (blocks + far + 8) * 8

    note = jnp.concatenate(
        [requested[0], jnp.broadcast_to(counts[:, None], (devices, 8))], axis=1
    )
    got = exchange(note.reshape(devices, 1, 16)).reshape(devices, 16)
    cells, width = coarse.shape
    home = call(
        home_kernel,
        shape(devices, 8, width),
        [ANY, ANY],
        [
            pltpu.SMEM(subdivided.shape, jnp.int32),
            pltpu.VMEM((cells, width), BF16),
            pltpu.VMEM((2, cells, 128), F32),
            pltpu.VMEM((2, far, 128), F32),
            pltpu.SemaphoreType.DMA((5,)),
        ],
        flops=2**30,
    )(subdivided, coarse)
    idx = (neighbours * 8).reshape(-1)

    leaving = call(roll_kernel, shape(devices, 8, 256), [VM, VM], limit=SMALL)(got, home)
    arrived = exchange(leaving)
    parent, send = call(
        parent_kernel,
        (shape(blocks, 256), shape(devices, 8, 256)),
        [VM, VM],
        [pltpu.VMEM((2, far, 128), F32)],
        limit=SMALL,
    )(got, arrived.reshape(far, 256))
    far_parent = exchange(send).reshape(far, 256)

    work = [
        pltpu.VMEM((table_rows, 128), F32),
        (pltpu.VMEM((blocks * 8, 128), F32),) * 2,
        pltpu.VMEM((8, blocks, 128), F32),
        pltpu.SMEM(idx.shape, jnp.int32),
        pltpu.VMEM(first_conv.shape, BF16),
        pltpu.VMEM((blocks, 1024), BF16),
    ]
    own = shape(8, blocks, 128, dtype=F32)
    child, total = call(own_kernel, (shape(blocks, 1024), own), [VM] * 3, flops=3 * 2**30, limit=SMALL)(
        parent, up_weight, first_conv
    )
    hidden, send = call(
        first_kernel,
        (shape(blocks, 1024), shape(devices, 8, 1024)),
        [ANY, VM, ANY, VM, VM, ANY, ANY],
        work
        + [
            pltpu.VMEM((2, far, 128), F32),
            pltpu.VMEM((blocks, 1024), BF16),
            pltpu.VMEM((devices, 8, 1024), BF16),
            pltpu.SemaphoreType.DMA((9,)),
        ],
        (ANY, ANY),
    )(idx, got, child, far_parent, up_weight, first_conv, total)
    far_hidden = exchange(send).reshape(far, 1024)
    total = call(own_second_kernel, own, [VM] * 3, flops=3 * 2**30, limit=SMALL)(child, hidden, second_conv)
    return tuple(
        call(
            second_kernel,
            (shape(blocks, 1024), shape(8, blocks, dtype=F32)),
            [ANY] * 5 + [VM],
            work + [pltpu.VMEM((far, 1024), BF16), pltpu.SemaphoreType.DMA((6,))],
        )(idx, hidden, far_hidden, second_conv, total, occupancy_weight.reshape(1, 128))
    )


def solution(mesh):
    rows = P(AXES, None)
    in_specs = (rows, P(AXES), rows, P(AXES, None, None), P(None, AXES), P(), P(), P(), P())
    out_specs = (rows, P(None, AXES))
    return jax.shard_map(body, mesh=mesh, in_specs=in_specs, out_specs=out_specs, check_vma=False)
```

```python
import functools

import jax
import jax.numpy as jnp
import numpy as np
from jax import lax
from jax.experimental import pallas as pl
from jax.experimental.pallas import tpu as pltpu
from jax.sharding import PartitionSpec as P

AXES = ("slab", "tile")
F32 = jnp.float32
BF16 = jnp.bfloat16
VMEM_LIMIT = 58 * 2**20
SMALL = 16 * 2**20
VM = pl.BlockSpec(memory_space=pltpu.VMEM)
ANY = pl.BlockSpec(memory_space=pl.ANY)
GROUP = 32


def axis_children(offset):
    if offset == -1:
        return ([1], [0])
    if offset == 1:
        return ([0], [1])
    return ([0, 1], [0, 1])


def neighbour_plan():
    plans = []
    for near in np.ndindex(3, 3, 3):
        near = [v - 1 for v in near]
        parts = [axis_children(v) for v in near]
        sources = [(a, b, c) for a in parts[0][0] for b in parts[1][0] for c in parts[2][0]]
        targets = [(a, b, c) for a in parts[0][1] for b in parts[1][1] for c in parts[2][1]]
        taps = []
        for s in sources:
            row = []
            for t in targets:
                o = [2 * near[i] + s[i] - t[i] for i in range(3)]
                row.append(9 * (o[0] + 1) + 3 * (o[1] + 1) + o[2] + 1)
            taps.append(row)
        code = lambda v: 4 * v[0] + 2 * v[1] + v[2]
        plans.append(([code(s) for s in sources], [code(t) for t in targets], taps))
    return plans


PLANS = neighbour_plan()


def tap_block(w_ref, tap):
    return w_ref[tap * 128 : (tap + 1) * 128, :]


def tap_matrix(w_ref, taps):
    return jnp.concatenate(
        [jnp.concatenate([tap_block(w_ref, t) for t in row], axis=1) for row in taps], axis=0
    )


def dot(a, b):
    return jnp.dot(a, b, preferred_element_type=F32)


def add_dots(left, plan, w_ref, total, fresh=False):
    sources, targets, taps = plan
    step = min(2, len(targets))
    for j in range(0, len(targets), step):
        part = dot(left, tap_matrix(w_ref, [row[j : j + step] for row in taps]))
        for k in range(step):
            piece = part[:, k * 128 : (k + 1) * 128]
            if fresh:
                total[targets[j + k]] = piece
            else:
                total[targets[j + k]] += piece


def add_neighbours(idx_ref, w_ref, table, picked, total):
    blocks = total.shape[1]

    def pick(t):
        into = picked[t % 2]
        for first in range(t * blocks, (t + 1) * blocks, GROUP):
            rows = [
                table[pl.ds(pl.multiple_of(idx_ref[first + u], 8), 8), :] for u in range(GROUP)
            ]
            at = (first - t * blocks) * 8
            for u in range(GROUP):
                into[at + u * 8 : at + u * 8 + 8, :] = rows[u]

    for t in range(-1, 26):

        def step(i, carry, t=t):
            if t + 1 < 26:
                pick(t + 1)
            if t >= 0:
                plan = PLANS[t if t < 13 else t + 1]
                near = picked[t % 2]
                left = [near[pl.ds(s, blocks, stride=8), :].astype(BF16) for s in plan[0]]
                add_dots(jnp.concatenate(left, axis=1), plan, w_ref, total)
            return carry

        lax.fori_loop(0, 1, step, 0)


def copies(pairs, sems):
    made = [pltpu.make_async_copy(a, b, sems.at[i]) for i, (a, b) in enumerate(pairs)]
    for copy in made:
        copy.start()
    return made


def fill_table(table, ref, base):
    rows = 128

    def some(i, carry):
        at = pl.ds(pl.multiple_of(i * rows, rows), rows)
        to = pl.multiple_of((base + i * rows) * 8, rows * 8)
        for q in range(8):
            table[pl.ds(to + q, rows, stride=8), :] = (
                ref[at, q * 128 : (q + 1) * 128].astype(F32)
            )
        return carry

    lax.fori_loop(0, ref.shape[0] // rows, some, 0)


def silu(x):
    half = 0.5 * x
    return half + half * jnp.tanh(half)


def home_kernel(sub_ref, coarse_ref, out_ref, place, raw, wide, rows, sems):
    devices = out_ref.shape[0]
    cells = coarse_ref.shape[0]
    part = cells // 4
    spot = pltpu.make_async_copy(sub_ref, place, sems.at[4])
    spot.start()
    loads = copies(
        [(coarse_ref.at[pl.ds(i * part, part)], raw.at[pl.ds(i * part, part)]) for i in range(4)],
        sems,
    )
    for i in range(4):
        loads[i].wait()

        def widen(j, carry, i=i):
            at = pl.ds(pl.multiple_of(i * part + j * 128, 128), 128)
            for half in range(2):
                wide[half, at, :] = raw[at, half * 128 : (half + 1) * 128].astype(F32)
            return carry

        lax.fori_loop(0, part // 128, widen, 0, unroll=2)
    spot.wait()

    def some(i, carry):
        first = i * 32
        k = first // devices
        to = lax.rem(first, devices) * 8 + k
        cells_here = [place[0, first + u] for u in range(32)]
        for half in range(2):
            got = [wide[half, pl.ds(c, 1), :] for c in cells_here]
            for u in range(32):
                rows[half, pl.ds(to + u * 8, 1), :] = got[u]
        return carry

    lax.fori_loop(0, devices * 8 // 32, some, 0)
    for half in range(2):
        out_ref[:, :, half * 128 : (half + 1) * 128] = (
            rows[half].astype(BF16).reshape(devices, 8, 128)
        )


def own_index():
    return lax.axis_index(AXES[0]) * lax.axis_size(AXES[1]) + lax.axis_index(AXES[1])


def roll_kernel(got_ref, home_ref, out_ref):
    devices = got_ref.shape[0]
    me = own_index()
    ids = lax.broadcasted_iota(jnp.int32, (devices, 1), 0)
    lower = jnp.sum(jnp.where(ids < me, got_ref[:, 8:9], 0))
    shift = lax.rem(lower, devices)

    def one(d, carry):
        src = lax.rem(d - shift + devices, devices)
        out_ref[d] = home_ref[src]
        return carry

    lax.fori_loop(0, devices, one, 0, unroll=8)


def select_rows(got_ref, source, scratch, out_ref, done=None):
    devices = got_ref.shape[0]
    blocks, width = source.shape
    lanes = lax.broadcasted_iota(jnp.int32, (devices, blocks), 1)
    pick = jnp.concatenate(
        [(got_ref[:, k : k + 1] == lanes).astype(BF16) for k in range(8)], axis=0
    )
    for c in range(0, width, 256):
        part = dot(pick, source[:, c : c + 256])
        for half in range(2):
            to = scratch.at[half]
            for k in range(8):
                to[pl.ds(k, devices, stride=8), :] = (
                    part[k * devices : (k + 1) * devices, half * 128 : (half + 1) * 128]
                )
            at = c + half * 128
            out_ref[:, :, at : at + 128] = to[...].astype(BF16).reshape(devices, 8, 128)
        if done is not None:
            done(c // 256, pl.ds(c, 256))


def parent_kernel(got_ref, arrived_ref, parent_ref, send_ref, scratch):
    devices = got_ref.shape[0]
    blocks = parent_ref.shape[0]
    me = own_index()
    cols = devices * 8
    home = lax.broadcasted_iota(jnp.int32, (devices, cols), 1) // 8
    row = lax.broadcasted_iota(jnp.int32, (devices, cols), 0)
    counts = got_ref[:, 8:9]
    lower = jnp.sum(jnp.where(row < home, counts, 0), axis=0, keepdims=True)
    upper = jnp.sum(jnp.where(row <= home, counts, 0), axis=0, keepdims=True)
    within = lax.broadcasted_iota(jnp.int32, (1, cols), 1) % 8
    slot = (lower - me + devices - 1) // devices + within
    slot = jnp.where(slot * devices + me < upper, slot, -1)
    pick = (lax.broadcasted_iota(jnp.int32, (blocks, cols), 0) == slot).astype(BF16)
    parent = dot(pick, arrived_ref[...]).astype(BF16)
    parent_ref[...] = parent
    select_rows(got_ref, parent, scratch, send_ref)


def own_kernel(parent_ref, up_ref, w_ref, child_ref, total_ref):
    child_ref[...] = silu(dot(parent_ref[...], up_ref[...])).astype(BF16)
    add_dots(child_ref[...], PLANS[13], w_ref, total_ref, fresh=True)


def own_second_kernel(child_ref, hidden_ref, w_ref, total_ref):
    add_dots(hidden_ref[...], PLANS[13], w_ref, total_ref, fresh=True)
    for q in range(8):
        total_ref[q] += child_ref[:, q * 128 : (q + 1) * 128].astype(F32)


def first_kernel(
    idx_ref, got_ref, child_ref, far_ref, up_ref, w_ref, total_ref,
    hidden_ref, send_ref,
    table, picked, total, idx, w, child, scratch, hidden, send, sems,
):
    blocks = child_ref.shape[0]
    far = far_ref.shape[0]
    rows = 512
    loads = copies(
        [(child_ref, child), (idx_ref, idx), (w_ref, w), (total_ref, total)], sems
    )

    def far_rows(i, carry):
        at = pl.ds(pl.multiple_of(i * rows, rows), rows)
        to = pl.multiple_of((blocks + i * rows) * 8, 8)
        made = silu(dot(far_ref[at, :], up_ref[...])).astype(BF16)
        for q in range(8):
            table[pl.ds(to + q, rows, stride=8), :] = made[:, q * 128 : (q + 1) * 128].astype(F32)
        return carry

    lax.fori_loop(0, far // rows, far_rows, 0)
    last = (blocks + far) * 8
    table[last : last + 8, :] = jnp.zeros((8, 128), F32)
    loads[0].wait()
    fill_table(table, child, 0)
    for load in loads[1:]:
        load.wait()
    add_neighbours(idx, w, table, picked, total)
    for q in range(8):
        hidden[:, q * 128 : (q + 1) * 128] = silu(total[q]).astype(BF16)
    leaving = [pltpu.make_async_copy(hidden, hidden_ref, sems.at[4])]
    leaving[0].start()

    def send_columns(number, columns):
        copy = pltpu.make_async_copy(
            send.at[:, :, columns], send_ref.at[:, :, columns], sems.at[5 + number]
        )
        copy.start()
        leaving.append(copy)

    select_rows(got_ref, hidden, scratch, send, send_columns)
    for copy in leaving:
        copy.wait()


def second_kernel(
    idx_ref, hidden_ref, far_ref, w_ref, total_ref, occ_ref,
    feature_ref, occupancy_ref,
    table, picked, total, idx, w, hidden, far, sems,
):
    blocks = hidden_ref.shape[0]
    rows = far_ref.shape[0]
    half = rows // 2
    loads = copies(
        [
            (hidden_ref, hidden),
            (far_ref.at[pl.ds(0, half)], far.at[pl.ds(0, half)]),
            (far_ref.at[pl.ds(half, half)], far.at[pl.ds(half, half)]),
            (idx_ref, idx),
            (w_ref, w),
            (total_ref, total),
        ],
        sems,
    )
    last = (blocks + rows) * 8
    table[last : last + 8, :] = jnp.zeros((8, 128), F32)
    loads[0].wait()
    fill_table(table, hidden, 0)
    for part in range(2):
        loads[1 + part].wait()
        fill_table(table, far.at[pl.ds(part * half, half)], blocks + part * half)
    for load in loads[3:]:
        load.wait()
    add_neighbours(idx, w, table, picked, total)
    for q in range(8):
        feature_ref[:, q * 128 : (q + 1) * 128] = total[q].astype(BF16)
    lane = lax.broadcasted_iota(jnp.int32, (8, 1024), 1) // 128
    row = lax.broadcasted_iota(jnp.int32, (8, 1024), 0)
    head = jnp.where(lane == row, jnp.concatenate([occ_ref[...].astype(F32)] * 8, axis=1), 0.0)
    occupancy_ref[...] = lax.dot_general(
        head.astype(BF16), feature_ref[...], (((1,), (1,)), ((), ())), preferred_element_type=F32
    )


def shape(*dims, dtype=BF16):
    return jax.ShapeDtypeStruct(dims, dtype)


def call(kernel, out_shape, in_specs, scratch=(), out_specs=None, flops=0, limit=VMEM_LIMIT):
    return pl.pallas_call(
        kernel,
        out_shape=out_shape,
        in_specs=in_specs,
        out_specs=out_specs or jax.tree.map(lambda _: VM, out_shape),
        scratch_shapes=list(scratch),
        compiler_params=pltpu.CompilerParams(vmem_limit_bytes=limit),
        cost_estimate=pl.CostEstimate(flops=flops, bytes_accessed=4 * 2**20, transcendentals=0),
    )


def exchange(x):
    return lax.all_to_all(x, AXES, split_axis=0, concat_axis=0, tiled=True)


def body(
    coarse, counts, subdivided, requested, neighbours,
    up_weight, first_conv, second_conv, occupancy_weight,
):
    devices = lax.axis_size(AXES)
    blocks = neighbours.shape[1]
    far = devices * 8
    table_rows = (blocks + far + 8) * 8

    note = jnp.concatenate(
        [requested[0], jnp.broadcast_to(counts[:, None], (devices, 8))], axis=1
    )
    got = exchange(note.reshape(devices, 1, 16)).reshape(devices, 16)
    cells, width = coarse.shape
    home = call(
        home_kernel,
        shape(devices, 8, width),
        [ANY, ANY],
        [
            pltpu.SMEM(subdivided.shape, jnp.int32),
            pltpu.VMEM((cells, width), BF16),
            pltpu.VMEM((2, cells, 128), F32),
            pltpu.VMEM((2, far, 128), F32),
            pltpu.SemaphoreType.DMA((5,)),
        ],
        flops=2**30,
        limit=SMALL + 8 * 2**20,
    )(subdivided, coarse)
    idx = (neighbours * 8).reshape(-1)

    leaving = call(roll_kernel, shape(devices, 8, 256), [VM, VM], limit=SMALL)(got, home)
    arrived = exchange(leaving)
    parent, send = call(
        parent_kernel,
        (shape(blocks, 256), shape(devices, 8, 256)),
        [VM, VM],
        [pltpu.VMEM((2, far, 128), F32)],
        limit=SMALL,
    )(got, arrived.reshape(far, 256))
    far_parent = exchange(send).reshape(far, 256)

    work = [
        pltpu.VMEM((table_rows, 128), F32),
        (pltpu.VMEM((blocks * 8, 128), F32),) * 2,
        pltpu.VMEM((8, blocks, 128), F32),
        pltpu.SMEM(idx.shape, jnp.int32),
        pltpu.VMEM(first_conv.shape, BF16),
        pltpu.VMEM((blocks, 1024), BF16),
    ]
    own = shape(8, blocks, 128, dtype=F32)
    child, total = call(own_kernel, (shape(blocks, 1024), own), [VM] * 3, flops=3 * 2**30, limit=SMALL)(
        parent, up_weight, first_conv
    )
    hidden, send = call(
        first_kernel,
        (shape(blocks, 1024), shape(devices, 8, 1024)),
        [ANY, VM, ANY, VM, VM, ANY, ANY],
        work
        + [
            pltpu.VMEM((2, far, 128), F32),
            pltpu.VMEM((blocks, 1024), BF16),
            pltpu.VMEM((devices, 8, 1024), BF16),
            pltpu.SemaphoreType.DMA((9,)),
        ],
        (ANY, ANY),
        limit=52 * 2**20,
    )(idx, got, child, far_parent, up_weight, first_conv, total)
    far_hidden = exchange(send).reshape(far, 1024)
    total = call(own_second_kernel, own, [VM] * 3, flops=3 * 2**30, limit=SMALL)(child, hidden, second_conv)
    return tuple(
        call(
            second_kernel,
            (shape(blocks, 1024), shape(8, blocks, dtype=F32)),
            [ANY] * 5 + [VM],
            work + [pltpu.VMEM((far, 1024), BF16), pltpu.SemaphoreType.DMA((6,))],
        )(idx, hidden, far_hidden, second_conv, total, occupancy_weight.reshape(1, 128))
    )


def solution(mesh):
    rows = P(AXES, None)
    in_specs = (rows, P(AXES), rows, P(AXES, None, None), P(None, AXES), P(), P(), P(), P())
    out_specs = (rows, P(None, AXES))
    return jax.shard_map(body, mesh=mesh, in_specs=in_specs, out_specs=out_specs, check_vma=False)
```

```python
import functools

import jax
import jax.numpy as jnp
import numpy as np
from jax import lax
from jax.experimental import pallas as pl
from jax.experimental.pallas import tpu as pltpu
from jax.sharding import PartitionSpec as P

AXES = ("slab", "tile")
F32 = jnp.float32
BF16 = jnp.bfloat16
VMEM_LIMIT = 58 * 2**20
SMALL = 16 * 2**20
VM = pl.BlockSpec(memory_space=pltpu.VMEM)
ANY = pl.BlockSpec(memory_space=pl.ANY)
GROUP = 32


def axis_children(offset):
    if offset == -1:
        return ([1], [0])
    if offset == 1:
        return ([0], [1])
    return ([0, 1], [0, 1])


def neighbour_plan():
    plans = []
    for near in np.ndindex(3, 3, 3):
        near = [v - 1 for v in near]
        parts = [axis_children(v) for v in near]
        sources = [(a, b, c) for a in parts[0][0] for b in parts[1][0] for c in parts[2][0]]
        targets = [(a, b, c) for a in parts[0][1] for b in parts[1][1] for c in parts[2][1]]
        taps = []
        for s in sources:
            row = []
            for t in targets:
                o = [2 * near[i] + s[i] - t[i] for i in range(3)]
                row.append(9 * (o[0] + 1) + 3 * (o[1] + 1) + o[2] + 1)
            taps.append(row)
        code = lambda v: 4 * v[0] + 2 * v[1] + v[2]
        plans.append(([code(s) for s in sources], [code(t) for t in targets], taps))
    return plans


PLANS = neighbour_plan()


def tap_block(w_ref, tap):
    return w_ref[tap * 128 : (tap + 1) * 128, :]


def tap_matrix(w_ref, taps):
    return jnp.concatenate(
        [jnp.concatenate([tap_block(w_ref, t) for t in row], axis=1) for row in taps], axis=0
    )


def dot(a, b):
    return jnp.dot(a, b, preferred_element_type=F32)


def add_dots(left, plan, w_ref, total, fresh=False):
    sources, targets, taps = plan
    step = min(2, len(targets))
    for j in range(0, len(targets), step):
        part = dot(left, tap_matrix(w_ref, [row[j : j + step] for row in taps]))
        for k in range(step):
            piece = part[:, k * 128 : (k + 1) * 128]
            if fresh:
                total[targets[j + k]] = piece
            else:
                total[targets[j + k]] += piece


def add_neighbours(idx_ref, w_ref, table, picked, total, late=()):
    blocks = total.shape[1]

    def pick(t):
        into = picked[t % 2]
        for first in range(t * blocks, (t + 1) * blocks, GROUP):
            rows = [
                table[pl.ds(pl.multiple_of(idx_ref[first + u], 8), 8), :] for u in range(GROUP)
            ]
            at = (first - t * blocks) * 8
            for u in range(GROUP):
                into[at + u * 8 : at + u * 8 + 8, :] = rows[u]

    for t in range(-1, 26):

        def step(i, carry, t=t):
            if t + 1 < 26:
                pick(t + 1)
            if t >= 0:
                plan = PLANS[t if t < 13 else t + 1]
                near = picked[t % 2]
                left = [near[pl.ds(s, blocks, stride=8), :].astype(BF16) for s in plan[0]]
                add_dots(jnp.concatenate(left, axis=1), plan, w_ref, total)
            return carry

        lax.fori_loop(0, 1, step, 0)
        if t < 0:
            for load in late:
                load.wait()


def copies(pairs, sems):
    made = [pltpu.make_async_copy(a, b, sems.at[i]) for i, (a, b) in enumerate(pairs)]
    for copy in made:
        copy.start()
    return made


def fill_table(table, ref, base):
    rows = 128

    def some(i, carry):
        at = pl.ds(pl.multiple_of(i * rows, rows), rows)
        to = pl.multiple_of((base + i * rows) * 8, rows * 8)
        for q in range(8):
            table[pl.ds(to + q, rows, stride=8), :] = (
                ref[at, q * 128 : (q + 1) * 128].astype(F32)
            )
        return carry

    lax.fori_loop(0, ref.shape[0] // rows, some, 0)


def silu(x):
    half = 0.5 * x
    return half + half * jnp.tanh(half)


def home_kernel(sub_ref, coarse_ref, out_ref, place, raw, wide, rows, sems):
    devices = out_ref.shape[0]
    cells = coarse_ref.shape[0]
    part = cells // 4
    spot = pltpu.make_async_copy(sub_ref, place, sems.at[4])
    spot.start()
    loads = copies(
        [(coarse_ref.at[pl.ds(i * part, part)], raw.at[pl.ds(i * part, part)]) for i in range(4)],
        sems,
    )
    for i in range(4):
        loads[i].wait()

        def widen(j, carry, i=i):
            at = pl.ds(pl.multiple_of(i * part + j * 128, 128), 128)
            for half in range(2):
                wide[half, at, :] = raw[at, half * 128 : (half + 1) * 128].astype(F32)
            return carry

        lax.fori_loop(0, part // 128, widen, 0, unroll=2)
    spot.wait()

    def some(i, carry):
        first = i * 32
        k = first // devices
        to = lax.rem(first, devices) * 8 + k
        cells_here = [place[0, first + u] for u in range(32)]
        for half in range(2):
            got = [wide[half, pl.ds(c, 1), :] for c in cells_here]
            for u in range(32):
                rows[half, pl.ds(to + u * 8, 1), :] = got[u]
        return carry

    lax.fori_loop(0, devices * 8 // 32, some, 0)
    for half in range(2):
        out_ref[:, :, half * 128 : (half + 1) * 128] = (
            rows[half].astype(BF16).reshape(devices, 8, 128)
        )


def own_index():
    return lax.axis_index(AXES[0]) * lax.axis_size(AXES[1]) + lax.axis_index(AXES[1])


def roll_kernel(got_ref, home_ref, out_ref):
    devices = got_ref.shape[0]
    me = own_index()
    ids = lax.broadcasted_iota(jnp.int32, (devices, 1), 0)
    lower = jnp.sum(jnp.where(ids < me, got_ref[:, 8:9], 0))
    shift = lax.rem(lower, devices)

    def one(d, carry):
        src = lax.rem(d - shift + devices, devices)
        out_ref[d] = home_ref[src]
        return carry

    lax.fori_loop(0, devices, one, 0, unroll=8)


def select_rows(got_ref, source, scratch, out_ref, done=None):
    devices = got_ref.shape[0]
    blocks, width = source.shape
    lanes = lax.broadcasted_iota(jnp.int32, (devices, blocks), 1)
    pick = jnp.concatenate(
        [(got_ref[:, k : k + 1] == lanes).astype(BF16) for k in range(8)], axis=0
    )
    for c in range(0, width, 256):
        part = dot(pick, source[:, c : c + 256])
        for half in range(2):
            to = scratch.at[half]
            for k in range(8):
                to[pl.ds(k, devices, stride=8), :] = (
                    part[k * devices : (k + 1) * devices, half * 128 : (half + 1) * 128]
                )
            at = c + half * 128
            out_ref[:, :, at : at + 128] = to[...].astype(BF16).reshape(devices, 8, 128)
        if done is not None:
            done(c // 256, pl.ds(c, 256))


def parent_kernel(got_ref, arrived_ref, parent_ref, send_ref, scratch):
    devices = got_ref.shape[0]
    blocks = parent_ref.shape[0]
    me = own_index()
    cols = devices * 8
    home = lax.broadcasted_iota(jnp.int32, (devices, cols), 1) // 8
    row = lax.broadcasted_iota(jnp.int32, (devices, cols), 0)
    counts = got_ref[:, 8:9]
    lower = jnp.sum(jnp.where(row < home, counts, 0), axis=0, keepdims=True)
    upper = jnp.sum(jnp.where(row <= home, counts, 0), axis=0, keepdims=True)
    within = lax.broadcasted_iota(jnp.int32, (1, cols), 1) % 8
    slot = (lower - me + devices - 1) // devices + within
    slot = jnp.where(slot * devices + me < upper, slot, -1)
    pick = (lax.broadcasted_iota(jnp.int32, (blocks, cols), 0) == slot).astype(BF16)
    parent = dot(pick, arrived_ref[...]).astype(BF16)
    parent_ref[...] = parent
    select_rows(got_ref, parent, scratch, send_ref)


def own_kernel(parent_ref, up_ref, w_ref, child_ref, total_ref):
    child_ref[...] = silu(dot(parent_ref[...], up_ref[...])).astype(BF16)
    add_dots(child_ref[...], PLANS[13], w_ref, total_ref, fresh=True)


def own_second_kernel(child_ref, hidden_ref, w_ref, total_ref):
    add_dots(hidden_ref[...], PLANS[13], w_ref, total_ref, fresh=True)
    for q in range(8):
        total_ref[q] += child_ref[:, q * 128 : (q + 1) * 128].astype(F32)


def first_kernel(
    idx_ref, got_ref, child_ref, far_ref, up_ref, w_ref, total_ref,
    hidden_ref, send_ref,
    table, picked, total, idx, w, child, scratch, hidden, send, sems,
):
    blocks = child_ref.shape[0]
    far = far_ref.shape[0]
    rows = 512
    loads = copies(
        [(child_ref, child), (idx_ref, idx), (w_ref, w), (total_ref, total)], sems
    )

    def far_rows(i, carry):
        at = pl.ds(pl.multiple_of(i * rows, rows), rows)
        to = pl.multiple_of((blocks + i * rows) * 8, 8)
        made = silu(dot(far_ref[at, :], up_ref[...])).astype(BF16)
        for q in range(8):
            table[pl.ds(to + q, rows, stride=8), :] = made[:, q * 128 : (q + 1) * 128].astype(F32)
        return carry

    lax.fori_loop(0, far // rows, far_rows, 0)
    last = (blocks + far) * 8
    table[last : last + 8, :] = jnp.zeros((8, 128), F32)
    loads[0].wait()
    fill_table(table, child, 0)
    for load in loads[1:]:
        load.wait()
    add_neighbours(idx, w, table, picked, total)
    for q in range(8):
        hidden[:, q * 128 : (q + 1) * 128] = silu(total[q]).astype(BF16)
    leaving = [pltpu.make_async_copy(hidden, hidden_ref, sems.at[4])]
    leaving[0].start()

    def send_columns(number, columns):
        copy = pltpu.make_async_copy(
            send.at[:, :, columns], send_ref.at[:, :, columns], sems.at[5 + number]
        )
        copy.start()
        leaving.append(copy)

    select_rows(got_ref, hidden, scratch, send, send_columns)
    for copy in leaving:
        copy.wait()


def second_kernel(
    idx_ref, hidden_ref, far_ref, w_ref, total_ref, occ_ref,
    feature_ref, occupancy_ref,
    table, picked, total, idx, w, hidden, far, sems,
):
    blocks = hidden_ref.shape[0]
    rows = far_ref.shape[0]
    part = rows // 4
    parts = [pl.ds(i * part, part) for i in range(4)]
    pairs = [(hidden_ref, hidden)] + [(far_ref.at[at], far.at[at]) for at in parts]
    loads = copies(pairs + [(idx_ref, idx)], sems)
    late = [
        pltpu.make_async_copy(w_ref, w, sems.at[6]),
        pltpu.make_async_copy(total_ref, total, sems.at[7]),
    ]
    for load in late:
        load.start()
    last = (blocks + rows) * 8
    table[last : last + 8, :] = jnp.zeros((8, 128), F32)
    loads[0].wait()
    fill_table(table, hidden, 0)
    for i in range(4):
        loads[1 + i].wait()
        fill_table(table, far.at[parts[i]], blocks + i * part)
    loads[5].wait()
    add_neighbours(idx, w, table, picked, total, late)
    for q in range(8):
        feature_ref[:, q * 128 : (q + 1) * 128] = total[q].astype(BF16)
    lane = lax.broadcasted_iota(jnp.int32, (8, 1024), 1) // 128
    row = lax.broadcasted_iota(jnp.int32, (8, 1024), 0)
    head = jnp.where(lane == row, jnp.concatenate([occ_ref[...].astype(F32)] * 8, axis=1), 0.0)
    occupancy_ref[...] = lax.dot_general(
        head.astype(BF16), feature_ref[...], (((1,), (1,)), ((), ())), preferred_element_type=F32
    )


def shape(*dims, dtype=BF16):
    return jax.ShapeDtypeStruct(dims, dtype)


def call(kernel, out_shape, in_specs, scratch=(), out_specs=None, flops=0, limit=VMEM_LIMIT):
    return pl.pallas_call(
        kernel,
        out_shape=out_shape,
        in_specs=in_specs,
        out_specs=out_specs or jax.tree.map(lambda _: VM, out_shape),
        scratch_shapes=list(scratch),
        compiler_params=pltpu.CompilerParams(vmem_limit_bytes=limit),
        cost_estimate=pl.CostEstimate(flops=flops, bytes_accessed=4 * 2**20, transcendentals=0),
    )


def exchange(x):
    return lax.all_to_all(x, AXES, split_axis=0, concat_axis=0, tiled=True)


def body(
    coarse, counts, subdivided, requested, neighbours,
    up_weight, first_conv, second_conv, occupancy_weight,
):
    devices = lax.axis_size(AXES)
    blocks = neighbours.shape[1]
    far = devices * 8
    table_rows = (blocks + far + 8) * 8

    note = jnp.concatenate(
        [requested[0], jnp.broadcast_to(counts[:, None], (devices, 8))], axis=1
    )
    got = exchange(note.reshape(devices, 1, 16)).reshape(devices, 16)
    cells, width = coarse.shape
    home = call(
        home_kernel,
        shape(devices, 8, width),
        [ANY, ANY],
        [
            pltpu.SMEM(subdivided.shape, jnp.int32),
            pltpu.VMEM((cells, width), BF16),
            pltpu.VMEM((2, cells, 128), F32),
            pltpu.VMEM((2, far, 128), F32),
            pltpu.SemaphoreType.DMA((5,)),
        ],
        flops=2**30,
        limit=SMALL + 8 * 2**20,
    )(subdivided, coarse)
    idx = (neighbours * 8).reshape(-1)

    leaving = call(roll_kernel, shape(devices, 8, 256), [VM, VM], limit=SMALL)(got, home)
    arrived = exchange(leaving)
    parent, send = call(
        parent_kernel,
        (shape(blocks, 256), shape(devices, 8, 256)),
        [VM, VM],
        [pltpu.VMEM((2, far, 128), F32)],
        limit=SMALL,
    )(got, arrived.reshape(far, 256))
    far_parent = exchange(send).reshape(far, 256)

    work = [
        pltpu.VMEM((table_rows, 128), F32),
        (pltpu.VMEM((blocks * 8, 128), F32),) * 2,
        pltpu.VMEM((8, blocks, 128), F32),
        pltpu.SMEM(idx.shape, jnp.int32),
        pltpu.VMEM(first_conv.shape, BF16),
        pltpu.VMEM((blocks, 1024), BF16),
    ]
    own = shape(8, blocks, 128, dtype=F32)
    child, total = call(own_kernel, (shape(blocks, 1024), own), [VM] * 3, flops=3 * 2**30, limit=SMALL)(
        parent, up_weight, first_conv
    )
    hidden, send = call(
        first_kernel,
        (shape(blocks, 1024), shape(devices, 8, 1024)),
        [ANY, VM, ANY, VM, VM, ANY, ANY],
        work
        + [
            pltpu.VMEM((2, far, 128), F32),
            pltpu.VMEM((blocks, 1024), BF16),
            pltpu.VMEM((devices, 8, 1024), BF16),
            pltpu.SemaphoreType.DMA((9,)),
        ],
        (ANY, ANY),
        limit=52 * 2**20,
    )(idx, got, child, far_parent, up_weight, first_conv, total)
    far_hidden = exchange(send).reshape(far, 1024)
    total = call(own_second_kernel, own, [VM] * 3, flops=3 * 2**30, limit=SMALL)(child, hidden, second_conv)
    return tuple(
        call(
            second_kernel,
            (shape(blocks, 1024), shape(8, blocks, dtype=F32)),
            [ANY] * 5 + [VM],
            work
            + [
                pltpu.VMEM((far, 1024), BF16),
                pltpu.SemaphoreType.DMA((8,)),
            ],
        )(idx, hidden, far_hidden, second_conv, total, occupancy_weight.reshape(1, 128))
    )


def solution(mesh):
    rows = P(AXES, None)
    in_specs = (rows, P(AXES), rows, P(AXES, None, None), P(None, AXES), P(), P(), P(), P())
    out_specs = (rows, P(None, AXES))
    return jax.shard_map(body, mesh=mesh, in_specs=in_specs, out_specs=out_specs, check_vma=False)
```
